512 devices in a mesh: dp: 16 (over z_hi, x), mp: 32 (over z_lo, y, core).
Axes of the slice: x: 4, y: 8, z: 8 (z_hi: 4, z_lo: 2; z = z_hi * 2 + z_lo), core: 2. Of those that a mesh axis runs over, the one named last changes fastest.
Arguments:
- partials: bfloat16 [16, 2048, 16384], P('dp', 'mp'), may hold values from -0.375 to 0.375
- owner: int32 [32], replicated, may hold values from 0 to 31, each once
- left_prev: float32 [32, 1024, 1024], P('mp', 'dp'), may hold values from -6 to 6
- right_prev: float32 [32, 1024, 1024], P('mp', 'dp'), may hold values from -6 to 6
- left_root: bfloat16 [32, 1024, 1024], P('mp', 'dp'), may hold values from -0.2 to 2.2
- right_root: bfloat16 [32, 1024, 1024], P('mp', 'dp'), may hold values from -0.2 to 2.2
Outputs:
- left_new: float32 [32, 1024, 1024], P('mp', 'dp')
- right_new: float32 [32, 1024, 1024], P('mp', 'dp')
- update: bfloat16 [32, 1024, 1024], P('mp', 'dp')
The draws below stay inside these ranges and needn't reach their ends.
Inputs may be any that keep to these rules, and one draw needn't show every extreme that they name: `owner`: each mp index owns exactly one block.
All inputs are finite; a program needn't handle non-finite values.
Results may differ from the reference program's by a relative error of at most 0.025.
Values may be sent and summed in bfloat16 or wider, within the bound.
No kernel may reach another device: no remote copies, remote signals or barrier semaphores. Data moves between devices by JAX's collectives and lax.ppermute only.
A program may use at most 64 MiB of HBM per device.

```python
import jax
import jax.numpy as jnp
from jax import lax

BS = 1024
NB = 32
BC = 16
ROWS = 2048
COLS = 16384
N_DP = 16


def root_like(key):
    key_normal = jax.random.fold_in(key, 0)
    key_diag = jax.random.fold_in(key, 2)
    shape = (NB, BS, BS)
    normal_part = jax.random.truncated_normal(key_normal, -4.0, 4.0, shape, jnp.float32)
    noise = normal_part
    symmetric = 0.02 * (noise + jnp.swapaxes(noise, 1, 2))
    diagonal = jnp.exp(jax.random.uniform(key_diag, (NB, BS, 1), jnp.float32, jnp.log(0.5), jnp.log(2.0)))
    rows_iota = lax_iota_rows()
    eye = (rows_iota[:, None] == rows_iota[None, :]).astype(jnp.float32)
    return (symmetric + eye[None, :, :] * diagonal).astype(jnp.bfloat16)


def lax_iota_rows():
    return jnp.arange(BS, dtype=jnp.int32)


def draw_left_root(key, part):
    key = jax.random.fold_in(key, 11)
    return root_like(key)


def draw_right_root(key, part):
    key = jax.random.fold_in(key, 23)
    return root_like(key)


def steps_of(stream_key, shape, cuts, least, largest):
    loudness = 1.0
    for dim, blocks in cuts:
        steps = jax.random.uniform(jax.random.fold_in(jax.random.fold_in(stream_key, 6), dim), (blocks,), jnp.float32, least / len(cuts), largest / len(cuts))
        loudness = loudness * jnp.repeat(jnp.exp(steps), shape[dim] // blocks).reshape((-1,) + (1,) * (len(shape) - 1 - dim))
    return loudness


def scatter_about(key, extent, spread, reach, cuts=(), kind=jnp.bfloat16):
    gain = steps_of(key, extent, cuts, -0.22, 0.18) if cuts else 1.0
    result = jax.random.normal(key, extent, jnp.float32) * spread * gain
    return jnp.minimum(jnp.maximum(result, -reach), reach).astype(kind)


def setup_inputs(seed: int = 0) -> dict:
    keys = jax.random.split(jax.random.key(seed), 7)
    partials = scatter_about(keys[0], (N_DP, ROWS, COLS), 0.0625, 0.375, ((0, 16), (1, 32)))
    owner = jax.random.permutation(keys[1], NB).astype(jnp.int32)
    left_prev = scatter_about(keys[2], (NB, BS, BS), 1.0, 6.0, ((0, 32), (1, 16)), jnp.float32)
    right_prev = scatter_about(keys[3], (NB, BS, BS), 1.0, 6.0, ((0, 32), (1, 16)), jnp.float32)
    left_root = draw_left_root(jax.random.fold_in(keys[6], 71), 0)
    right_root = draw_right_root(jax.random.fold_in(keys[6], 71), 0)
    return {"partials": partials, "owner": owner, "left_prev": left_prev, "right_prev": right_prev, "left_root": left_root, "right_root": right_root}


decay_rate = 0.95


def reference(partials, owner, left_prev, right_prev, left_root, right_root):
    def accumulate(running, layer):
        return running + layer.astype(jnp.float32), None

    summed, _ = lax.scan(accumulate, jnp.zeros(partials.shape[1:], jnp.float32), partials)
    grad = summed.astype(jnp.bfloat16)
    blocks = jnp.arange(NB, dtype=jnp.int32)
    holder = jnp.sum(jnp.where(owner[None, :] == blocks[:, None], blocks[None, :], 0), axis=1).astype(jnp.int32)

    def per_owner(owner_slot):
        block_index = holder[owner_slot]
        row_start = (block_index // BC) * BS
        col_start = (block_index % BC) * BS
        grad_block = lax.dynamic_slice(grad, (row_start.astype(jnp.int32), col_start.astype(jnp.int32)), (BS, BS))
        left_gram = jnp.dot(grad_block, grad_block.T, preferred_element_type=jnp.float32)
        right_gram = jnp.dot(grad_block.T, grad_block, preferred_element_type=jnp.float32)
        left_out = decay_rate * left_prev[owner_slot] + (1.0 - decay_rate) * left_gram
        right_out = decay_rate * right_prev[owner_slot] + (1.0 - decay_rate) * right_gram
        left_half = jnp.dot(left_root[owner_slot], grad_block, preferred_element_type=jnp.float32).astype(jnp.bfloat16)
        precond = jnp.dot(left_half, right_root[owner_slot], preferred_element_type=jnp.float32).astype(jnp.bfloat16)
        return left_out, right_out, precond

    left_new, right_new, update = lax.map(per_owner, blocks)
    return (left_new, right_new, update)
```

```python
import jax
import jax.numpy as jnp
from jax import lax
from jax.experimental import pallas as pl
from jax.experimental.pallas import tpu as pltpu
from jax.sharding import Mesh
from jax.sharding import PartitionSpec as P

decay_rate = 0.95
DP = ("zh", "x")
MP = ("zl", "y", "c")
NX = 4
NZ = 4
VMEM_LIMIT = 32 * 1024 * 1024


def call(kernel, out_shape, **kw):
    return pl.pallas_call(
        kernel,
        out_shape=out_shape,
        compiler_params=pltpu.CompilerParams(vmem_limit_bytes=VMEM_LIMIT),
        **kw,
    )


def sum_x_kernel(got_ref, out_ref):
    _, n_blocks, _, width = out_ref.shape
    for c in range(n_blocks):
        for z in range(NZ):
            cols = slice((c * NZ + z) * width, (c * NZ + z + 1) * width)
            total = got_ref[0, :, cols].astype(jnp.float32)
            for src in range(1, NX):
                total += got_ref[src, :, cols].astype(jnp.float32)
            out_ref[z, c] = total.astype(out_ref.dtype)


def route_kernel(owner_ref, got_ref, out_ref):
    n_blocks = got_ref.shape[1]
    first = lax.axis_index("zl") * n_blocks
    out_ref[...] = jnp.zeros_like(out_ref)
    for c in range(n_blocks):
        total = got_ref[0, c].astype(jnp.float32)
        for src in range(1, NZ):
            total += got_ref[src, c].astype(jnp.float32)
        out_ref[owner_ref[first + c]] = total.astype(out_ref.dtype)


def select_kernel(owner_ref, got_ref, mine_ref):
    n = mine_ref.shape[0]
    me = lax.axis_index(MP)
    row = jnp.int32(0)
    for b in range(n, 2 * n):
        row += (owner_ref[b] == me).astype(jnp.int32)
    mine_ref[...] = got_ref[pl.ds(row * n, n)]


def copies_kernel(one_ref, out_ref):
    out_ref[0] = one_ref[...]


def root_kernel(got_ref, out_ref):
    depth = got_ref.shape[2]
    for z in range(NZ):
        for x in range(NX):
            out_ref[pl.ds((z * NX + x) * depth, depth), :] = got_ref[x, z]


def product_kernel(pieces_ref, right_root_ref, left_root_hbm, left_prev_hbm, right_prev_hbm,
                   left_hbm, right_hbm, update_hbm,
                   g_ref, left_root, left_prev, right_prev, gram_ref, left_new, right_new, update, sems):
    d = lax.axis_index("zh") * NX + lax.axis_index("x")
    loads = [
        pltpu.make_async_copy(a, b, sems.at[i])
        for i, (a, b) in enumerate(
            ((left_root_hbm, left_root), (left_prev_hbm, left_prev), (right_prev_hbm, right_prev))
        )
    ]
    stores = [
        pltpu.make_async_copy(a, b, sems.at[3 + i])
        for i, (a, b) in enumerate(((left_new, left_hbm), (right_new, right_hbm), (update, update_hbm)))
    ]
    for c in loads:
        c.start()
    n_src, high, width = pieces_ref.shape[2:]
    share = left_prev.shape[0]
    for z in range(NZ):
        for x in range(NX):
            for s in range(n_src):
                g_ref[pl.ds((s * NX + x) * high, high), pl.ds(z * width, width)] = pieces_ref[x, z, s]
    rows = g_ref[pl.ds(pl.multiple_of(d * share, share), share), :]
    g = g_ref[...]
    left_gram = lax.dot_general(rows, g, (((1,), (1,)), ((), ())), preferred_element_type=jnp.float32)
    for c in loads:
        c.wait()
    left_new[...] = decay_rate * left_prev[...] + (1.0 - decay_rate) * left_gram
    stores[0].start()
    pair = g_ref[:, pl.ds(pl.multiple_of((d // 2) * 2 * share, 2 * share), 2 * share)]
    gram_ref[...] = lax.dot_general(pair, g, (((0,), (0,)), ((), ())), preferred_element_type=jnp.float32)
    right_gram = gram_ref[pl.ds(pl.multiple_of(lax.rem(d, 2) * share, share), share), :]
    right_new[...] = decay_rate * right_prev[...] + (1.0 - decay_rate) * right_gram
    stores[1].start()
    half = jnp.dot(left_root[...], g, preferred_element_type=jnp.float32).astype(jnp.bfloat16)
    update[...] = jnp.dot(half, right_root_ref[...], preferred_element_type=jnp.float32).astype(update.dtype)
    stores[2].start()
    for c in stores:
        c.wait()


def on_device(partials, owner, left_prev, right_prev, left_root, right_root):
    bf16, f32 = jnp.bfloat16, jnp.float32
    part = partials[0]
    rows, cols = part.shape
    order = left_prev.shape[2]
    share = left_prev.shape[1]
    n_blocks = cols // order
    n_mp = lax.axis_size(MP)
    high = rows // NX
    width = order // NZ
    piece = (n_blocks, high, width)
    vmem = pl.BlockSpec(memory_space=pltpu.VMEM)
    smem = pl.BlockSpec(memory_space=pltpu.SMEM)
    anywhere = pl.BlockSpec(memory_space=pl.ANY)
    shape = jax.ShapeDtypeStruct

    root_z = lax.all_gather(right_root[0], "zh")
    got = lax.all_to_all(part.reshape(NX, high, cols), "x", 0, 0, tiled=True)
    got, root_z = lax.optimization_barrier((got, root_z))
    root_xz = lax.all_gather(root_z, "x")
    cut = 4
    sums = call(
        sum_x_kernel,
        shape((NZ,) + piece, bf16),
        grid=(cut,),
        in_specs=[pl.BlockSpec((NX, high, cols // cut), lambda i: (0, 0, i))],
        out_specs=pl.BlockSpec((NZ, n_blocks // cut, high, width), lambda i: (0, i, 0, 0)),
    )(got)
    got = lax.all_to_all(sums, "zh", 0, 0, tiled=True)
    routed = call(
        route_kernel, shape((n_mp, high, width), bf16), in_specs=[smem, vmem], out_specs=vmem
    )(owner, got)
    got = lax.all_to_all(routed, MP, 0, 0, tiled=True)
    mine = call(select_kernel, shape(piece, bf16), in_specs=[smem, vmem], out_specs=vmem)(owner, got)
    column = lax.all_gather(mine, "zh")
    copies = call(
        copies_kernel,
        shape((NX, NZ) + piece, bf16),
        grid=(NX,),
        in_specs=[pl.BlockSpec((NZ,) + piece, lambda i: (0, 0, 0, 0))],
        out_specs=pl.BlockSpec((1, NZ) + piece, lambda i: (i, 0, 0, 0, 0)),
    )(column)
    pieces = lax.all_to_all(copies, "x", 0, 0, tiled=True)
    root = call(root_kernel, shape((order, order), bf16), in_specs=[vmem], out_specs=vmem)(root_xz)
    left_new, right_new, update = call(
        product_kernel,
        (shape((share, order), f32), shape((share, order), f32), shape((share, order), bf16)),
        in_specs=[vmem, vmem, anywhere, anywhere, anywhere],
        out_specs=(anywhere, anywhere, anywhere),
        scratch_shapes=[
            pltpu.VMEM((order, order), bf16),
            pltpu.VMEM((share, order), bf16),
            pltpu.VMEM((share, order), f32),
            pltpu.VMEM((share, order), f32),
            pltpu.VMEM((2 * share, order), f32),
            pltpu.VMEM((share, order), f32),
            pltpu.VMEM((share, order), f32),
            pltpu.VMEM((share, order), bf16),
            pltpu.SemaphoreType.DMA((6,)),
        ],
    )(pieces, root, left_root[0], left_prev[0], right_prev[0])
    return left_new[None], right_new[None], update[None]


def solution(mesh):
    cut = Mesh(mesh.devices.reshape(NZ, NX, 2, 8, 2), DP + MP)
    spread = P(MP, DP, None)
    return jax.shard_map(
        on_device,
        mesh=cut,
        in_specs=(P(DP, MP, None), P(), spread, spread, spread, spread),
        out_specs=(spread, spread, spread),
        check_vma=False,
    )
```

```python
import jax
import jax.numpy as jnp
from jax import lax
from jax.experimental import pallas as pl
from jax.experimental.pallas import tpu as pltpu
from jax.sharding import Mesh
from jax.sharding import PartitionSpec as P

decay_rate = 0.95
DP = ("zh", "x")
MP = ("zl", "y", "c")
NX = 4
NZ = 4
NL = 2
VMEM_LIMIT = 32 * 1024 * 1024


def call(kernel, out_shape, **kw):
    return pl.pallas_call(
        kernel,
        out_shape=out_shape,
        compiler_params=pltpu.CompilerParams(vmem_limit_bytes=VMEM_LIMIT),
        **kw,
    )


def sum_x_kernel(got_ref, out_ref):
    n_z, n_blocks, _, width = out_ref.shape
    for c in range(n_blocks):
        for z in range(n_z):
            cols = slice((c * n_z + z) * width, (c * n_z + z + 1) * width)
            total = got_ref[0, :, cols].astype(jnp.float32)
            for src in range(1, NX):
                total += got_ref[src, :, cols].astype(jnp.float32)
            out_ref[z, c] = total.astype(out_ref.dtype)


def route_kernel(owner_ref, got_ref, out_ref):
    n_blocks = got_ref.shape[1]
    for r in range(NL):
        for c in range(n_blocks):
            total = got_ref[r, c].astype(jnp.float32)
            for src in range(1, NZ):
                total += got_ref[src * NL + r, c].astype(jnp.float32)
            out_ref[owner_ref[r * n_blocks + c]] = total.astype(out_ref.dtype)


def copies_kernel(one_ref, out_ref):
    out_ref[0] = one_ref[...]


def pair_kernel(one_ref, two_ref, out_ref):
    out_ref[0] = one_ref[...]
    out_ref[1] = two_ref[...]


def product_kernel(*refs):
    pieces_ref = refs[0]
    (pair_ref, swap_ref, left_root_hbm, left_prev_hbm, right_prev_hbm, left_hbm, right_hbm, update_hbm,
     g_ref, root_ref, left_root, left_prev, right_prev, gram_ref, left_new, right_new, update, sems) = refs[1:]
    zh = lax.axis_index("zh")
    x_me = lax.axis_index("x")
    d = zh * NX + x_me
    share = left_prev.shape[0]
    loads = [
        pltpu.make_async_copy(a, b, sems.at[i])
        for i, (a, b) in enumerate(
            ((left_root_hbm, left_root), (left_prev_hbm, left_prev), (right_prev_hbm, right_prev))
        )
    ]
    stores = [
        pltpu.make_async_copy(a, b, sems.at[3 + i])
        for i, (a, b) in enumerate(((left_new, left_hbm), (right_new, right_hbm), (update, update_hbm)))
    ]
    for c in loads:
        c.start()
    n_piece, high, width = pieces_ref.shape[2:]
    n_src = n_piece // NL
    for j in range(NX):
        for z in range(NZ):
            for p in range(n_piece):
                at = (p % n_src * NX + j) * high
                to = (z * NL + p // n_src) * width
                g_ref[at : at + high, to : to + width] = pieces_ref[j, z, p]
    rows = g_ref[pl.ds(pl.multiple_of(d * share, share), share), :]
    g = g_ref[...]
    left_gram = lax.dot_general(rows, g, (((1,), (1,)), ((), ())), preferred_element_type=jnp.float32)
    for c in loads:
        c.wait()
    left_new[...] = decay_rate * left_prev[...] + (1.0 - decay_rate) * left_gram
    stores[0].start()
    pair = g_ref[:, pl.ds(pl.multiple_of((d // 2) * 2 * share, 2 * share), 2 * share)]
    gram_ref[...] = lax.dot_general(pair, g, (((0,), (0,)), ((), ())), preferred_element_type=jnp.float32)
    right_gram = gram_ref[pl.ds(pl.multiple_of(lax.rem(d, 2) * share, share), share), :]
    right_new[...] = decay_rate * right_prev[...] + (1.0 - decay_rate) * right_gram
    stores[1].start()
    half = jnp.dot(left_root[...], g, preferred_element_type=jnp.float32).astype(jnp.bfloat16)
    for j, (ref, part) in enumerate(((pair_ref, 0), (pair_ref, 1), (swap_ref, 1), (swap_ref, 0))):
        for z in range(NZ):
            at = pl.multiple_of((z * NX + lax.bitwise_xor(x_me, j)) * share, share)
            root_ref[pl.ds(at, share), :] = ref[part, z * share : (z + 1) * share, :]
    update[...] = jnp.dot(half, root_ref[...], preferred_element_type=jnp.float32).astype(update.dtype)
    stores[2].start()
    for c in stores:
        c.wait()


def on_device(partials, owner, left_prev, right_prev, left_root, right_root):
    bf16, f32 = jnp.bfloat16, jnp.float32
    part = partials[0]
    rows, cols = part.shape
    order = left_prev.shape[2]
    share = left_prev.shape[1]
    n_blocks = cols // order
    n_mp = lax.axis_size(MP)
    high = rows // NX
    width = order // (NZ * NL)
    piece = (n_blocks, high, width)
    vmem = pl.BlockSpec(memory_space=pltpu.VMEM)
    smem = pl.BlockSpec(memory_space=pltpu.SMEM)
    anywhere = pl.BlockSpec(memory_space=pl.ANY)
    shape = jax.ShapeDtypeStruct

    swaps = {k: [(i, i ^ k) for i in range(NX)] for k in range(1, NX)}

    root_z = lax.all_gather(right_root[0], "zh", tiled=True)
    got = lax.all_to_all(part.reshape(NX, high, cols), "x", 0, 0, tiled=True)
    got, root_z = lax.optimization_barrier((got, root_z))
    cut = 4
    sums = call(
        sum_x_kernel,
        shape((NZ * NL,) + piece, bf16),
        grid=(cut,),
        in_specs=[pl.BlockSpec((NX, high, cols // cut), lambda i: (0, 0, i))],
        out_specs=pl.BlockSpec((NZ * NL, n_blocks // cut, high, width), lambda i: (0, i, 0, 0)),
    )(got)
    root_next = lax.ppermute(root_z, "x", swaps[1])
    got = lax.all_to_all(sums, ("zh", "zl"), 0, 0, tiled=True)
    got, root_z, root_next = lax.optimization_barrier((got, root_z, root_next))
    routed = call(
        route_kernel, shape((n_mp, high, width), bf16), in_specs=[smem, vmem], out_specs=vmem
    )(owner, got)
    root_pair = call(
        pair_kernel, shape((2,) + root_z.shape, bf16), in_specs=[vmem, vmem], out_specs=vmem
    )(root_z, root_next)
    routed, root_pair = lax.optimization_barrier((routed, root_pair))
    root_swap = lax.ppermute(root_pair, "x", swaps[3])
    mine = lax.all_to_all(routed, MP, 0, 0, tiled=True)
    column = lax.all_gather(mine, "zh")
    column, root_swap = lax.optimization_barrier((column, root_swap))
    copies = call(
        copies_kernel,
        shape((NX,) + column.shape, bf16),
        grid=(NX,),
        in_specs=[pl.BlockSpec(column.shape, lambda i: (0, 0, 0, 0))],
        out_specs=pl.BlockSpec((1,) + column.shape, lambda i: (i, 0, 0, 0, 0)),
    )(column)
    pieces = lax.all_to_all(copies, "x", 0, 0, tiled=True)
    left_new, right_new, update = call(
        product_kernel,
        (shape((share, order), f32), shape((share, order), f32), shape((share, order), bf16)),
        in_specs=[vmem] * 3 + [anywhere] * 3,
        out_specs=(anywhere, anywhere, anywhere),
        scratch_shapes=[
            pltpu.VMEM((order, order), bf16),
            pltpu.VMEM((order, order), bf16),
            pltpu.VMEM((share, order), bf16),
            pltpu.VMEM((share, order), f32),
            pltpu.VMEM((share, order), f32),
            pltpu.VMEM((2 * share, order), f32),
            pltpu.VMEM((share, order), f32),
            pltpu.VMEM((share, order), f32),
            pltpu.VMEM((share, order), bf16),
            pltpu.SemaphoreType.DMA((6,)),
        ],
    )(pieces, root_pair, root_swap, left_root[0], left_prev[0], right_prev[0])
    return left_new[None], right_new[None], update[None]


def solution(mesh):
    cut = Mesh(mesh.devices.reshape(NZ, NX, 2, 8, 2), DP + MP)
    spread = P(MP, DP, None)
    return jax.shard_map(
        on_device,
        mesh=cut,
        in_specs=(P(DP, MP, None), P(), spread, spread, spread, spread),
        out_specs=(spread, spread, spread),
        check_vma=False,
    )
```

```python
import jax
import jax.numpy as jnp
from jax import lax
from jax.experimental import pallas as pl
from jax.experimental.pallas import tpu as pltpu
from jax.sharding import Mesh
from jax.sharding import PartitionSpec as P

decay_rate = 0.95
DP = ("zh", "x")
MP = ("zl", "y", "c")
NX = 4
NZ = 4
NL = 2
VMEM_LIMIT = 32 * 1024 * 1024


def call(kernel, out_shape, **kw):
    return pl.pallas_call(
        kernel,
        out_shape=out_shape,
        compiler_params=pltpu.CompilerParams(vmem_limit_bytes=VMEM_LIMIT),
        **kw,
    )


def sum_x_kernel(got_ref, out_ref):
    n_here, n_blocks, _, width = out_ref.shape
    first = pl.program_id(0) * n_here
    for c in range(n_blocks):
        for z in range(n_here):
            cols = pl.ds(pl.multiple_of((c * NZ * NL + first + z) * width, width), width)
            total = got_ref[0, :, cols].astype(jnp.float32)
            for src in range(1, NX):
                total += got_ref[src, :, cols].astype(jnp.float32)
            out_ref[z, c] = total.astype(out_ref.dtype)


def route_kernel(owner_ref, got_ref, out_ref):
    n_blocks = got_ref.shape[1]
    for r in range(NL):
        for c in range(n_blocks):
            total = got_ref[r, c].astype(jnp.float32)
            for src in range(1, NZ):
                total += got_ref[src * NL + r, c].astype(jnp.float32)
            out_ref[owner_ref[r * n_blocks + c]] = total.astype(out_ref.dtype)


def halves_kernel(column_ref, low_ref, top_ref):
    n = low_ref.shape[0]
    low_ref[...] = column_ref[:n]
    top_ref[...] = column_ref[n:]


def pair_kernel(one_ref, two_ref, out_ref):
    out_ref[0] = one_ref[...]
    out_ref[1] = two_ref[...]


def root_kernel(pair_ref, swap_ref, root_ref):
    x_me = lax.axis_index("x")
    share = pair_ref.shape[1] // NZ
    for j, (ref, part) in enumerate(((pair_ref, 0), (pair_ref, 1), (swap_ref, 1), (swap_ref, 0))):
        for z in range(NZ):
            at = pl.multiple_of((z * NX + lax.bitwise_xor(x_me, j)) * share, share)
            root_ref[pl.ds(at, share), :] = ref[part, z * share : (z + 1) * share, :]


def product_kernel(*refs):
    piece_refs = refs[: 2 * NX]
    (root_ref, left_root_hbm, left_prev_hbm, right_prev_hbm, left_hbm, right_hbm, update_hbm,
     g_ref, stack_ref, left_prev, right_prev, pair_ref, both_ref, left_new, right_new, update, sems) = refs[2 * NX :]
    zh = lax.axis_index("zh")
    x_me = lax.axis_index("x")
    d = zh * NX + x_me
    share = left_prev.shape[0]
    loads = [
        pltpu.make_async_copy(a, b, sems.at[i])
        for i, (a, b) in enumerate(
            ((left_root_hbm, stack_ref.at[:share]), (left_prev_hbm, left_prev), (right_prev_hbm, right_prev))
        )
    ]
    stores = [
        pltpu.make_async_copy(a, b, sems.at[3 + i])
        for i, (a, b) in enumerate(((left_new, left_hbm), (right_new, right_hbm), (update, update_hbm)))
    ]
    for c in loads:
        c.start()
    n_half, n_piece, high, width = piece_refs[0].shape
    n_src = n_piece // NL
    for j in range(NX):
        x = lax.bitwise_xor(x_me, j)
        for z in range(NZ):
            ref = piece_refs[2 * j + z // n_half]
            for p in range(n_piece):
                at = pl.multiple_of((p % n_src * NX + x) * high, high)
                to = (z * NL + p // n_src) * width
                g_ref[pl.ds(at, high), to : to + width] = ref[z % n_half, p]
    rows = g_ref[pl.ds(pl.multiple_of(d * share, share), share), :]
    g = g_ref[...]
    left_gram = lax.dot_general(rows, g, (((1,), (1,)), ((), ())), preferred_element_type=jnp.float32)
    for c in loads:
        c.wait()
    left_new[...] = decay_rate * left_prev[...] + (1.0 - decay_rate) * left_gram
    stores[0].start()
    pair = g_ref[:, pl.ds(pl.multiple_of((d // 2) * 2 * share, 2 * share), 2 * share)]
    pair_ref[...] = pair.T
    stack_ref[share:, :] = pair_ref[pl.ds(pl.multiple_of(lax.rem(d, 2) * share, share), share), :]
    both_ref[...] = jnp.dot(stack_ref[...], g, preferred_element_type=jnp.float32)
    right_new[...] = decay_rate * right_prev[...] + (1.0 - decay_rate) * both_ref[share:, :]
    stores[1].start()
    half = both_ref[:share, :].astype(jnp.bfloat16)
    update[...] = jnp.dot(half, root_ref[...], preferred_element_type=jnp.float32).astype(update.dtype)
    stores[2].start()
    for c in stores:
        c.wait()


def on_device(partials, owner, left_prev, right_prev, left_root, right_root):
    bf16, f32 = jnp.bfloat16, jnp.float32
    part = partials[0]
    rows, cols = part.shape
    order = left_prev.shape[2]
    share = left_prev.shape[1]
    n_blocks = cols // order
    n_mp = lax.axis_size(MP)
    high = rows // NX
    width = order // (NZ * NL)
    piece = (n_blocks, high, width)
    vmem = pl.BlockSpec(memory_space=pltpu.VMEM)
    smem = pl.BlockSpec(memory_space=pltpu.SMEM)
    anywhere = pl.BlockSpec(memory_space=pl.ANY)
    shape = jax.ShapeDtypeStruct

    swaps = {k: [(i, i ^ k) for i in range(NX)] for k in range(1, NX)}

    root_z = lax.all_gather(right_root[0], "zh", tiled=True)
    got = lax.all_to_all(part.reshape(NX, high, cols), "x", 0, 0, tiled=True)
    got, root_z = lax.optimization_barrier((got, root_z))
    cut = 4
    sums = call(
        sum_x_kernel,
        shape((NZ * NL,) + piece, bf16),
        grid=(cut,),
        in_specs=[pl.BlockSpec((NX, high, cols), lambda i: (0, 0, 0))],
        out_specs=pl.BlockSpec((NZ * NL // cut,) + piece, lambda i: (i, 0, 0, 0)),
    )(got)
    root_next = lax.ppermute(root_z, "x", swaps[1])
    got = lax.all_to_all(sums, ("zh", "zl"), 0, 0, tiled=True)
    got, root_z, root_next = lax.optimization_barrier((got, root_z, root_next))
    routed = call(
        route_kernel, shape((n_mp, high, width), bf16), in_specs=[smem, vmem], out_specs=vmem
    )(owner, got)
    root_pair = call(
        pair_kernel, shape((2,) + root_z.shape, bf16), in_specs=[vmem, vmem], out_specs=vmem
    )(root_z, root_next)
    routed, root_pair = lax.optimization_barrier((routed, root_pair))
    root_swap = lax.ppermute(root_pair, "x", swaps[3])
    mine = lax.all_to_all(routed, MP, 0, 0, tiled=True)
    column = lax.all_gather(mine, "zh")
    column, root_swap = lax.optimization_barrier((column, root_swap))
    low, top = call(
        halves_kernel, (shape((NZ // 2,) + column.shape[1:], bf16),) * 2, in_specs=[vmem], out_specs=(vmem, vmem)
    )(column.reshape((NZ, n_mp) + piece[1:]))
    low_1 = lax.ppermute(low, "x", swaps[1])
    top_3 = lax.ppermute(top, "x", swaps[3])
    top_1 = lax.ppermute(top, "x", swaps[1])
    low_3 = lax.ppermute(low, "x", swaps[3])
    low_2 = lax.ppermute(low_1, "x", swaps[3])
    top_2 = lax.ppermute(top_3, "x", swaps[1])
    pieces = [low, top, low_1, top_1, low_2, top_2, low_3, top_3]
    root = call(root_kernel, shape((order, order), bf16), in_specs=[vmem, vmem], out_specs=vmem)(root_pair, root_swap)
    left_new, right_new, update = call(
        product_kernel,
        (shape((share, order), f32), shape((share, order), f32), shape((share, order), bf16)),
        in_specs=[vmem] * (2 * NX + 1) + [anywhere] * 3,
        out_specs=(anywhere, anywhere, anywhere),
        scratch_shapes=[
            pltpu.VMEM((order, order), bf16),
            pltpu.VMEM((2 * share, order), bf16),
            pltpu.VMEM((share, order), f32),
            pltpu.VMEM((share, order), f32),
            pltpu.VMEM((2 * share, order), bf16),
            pltpu.VMEM((2 * share, order), f32),
            pltpu.VMEM((share, order), f32),
            pltpu.VMEM((share, order), f32),
            pltpu.VMEM((share, order), bf16),
            pltpu.SemaphoreType.DMA((6,)),
        ],
    )(*pieces, root, left_root[0], left_prev[0], right_prev[0])
    return left_new[None], right_new[None], update[None]


def solution(mesh):
    cut = Mesh(mesh.devices.reshape(NZ, NX, 2, 8, 2), DP + MP)
    spread = P(MP, DP, None)
    return jax.shard_map(
        on_device,
        mesh=cut,
        in_specs=(P(DP, MP, None), P(), spread, spread, spread, spread),
        out_specs=(spread, spread, spread),
        check_vma=False,
    )
```

```python
import jax
import jax.numpy as jnp
from jax import lax
from jax.experimental import pallas as pl
from jax.experimental.pallas import tpu as pltpu
from jax.sharding import Mesh
from jax.sharding import PartitionSpec as P

decay_rate = 0.95
DP = ("zh", "x")
MP = ("zl", "y", "c")
NX = 4
NZ = 4
NL = 2
VMEM_LIMIT = 32 * 1024 * 1024


def call(kernel, out_shape, **kw):
    return pl.pallas_call(
        kernel,
        out_shape=out_shape,
        compiler_params=pltpu.CompilerParams(vmem_limit_bytes=VMEM_LIMIT),
        **kw,
    )


def sum_x_kernel(got_ref, out_ref):
    n_here, n_blocks, _, width = out_ref.shape
    first = pl.program_id(0) * n_here
    for c in range(n_blocks):
        for z in range(n_here):
            cols = pl.ds(pl.multiple_of((c * NZ * NL + first + z) * width, width), width)
            total = got_ref[0, :, cols].astype(jnp.float32)
            for src in range(1, NX):
                total += got_ref[src, :, cols].astype(jnp.float32)
            out_ref[z, c] = total.astype(out_ref.dtype)


def route_kernel(owner_ref, got_ref, out_ref):
    n_blocks = got_ref.shape[1]
    for r in range(NL):
        for c in range(n_blocks):
            total = got_ref[r, c].astype(jnp.float32)
            for src in range(1, NZ):
                total += got_ref[src * NL + r, c].astype(jnp.float32)
            owner = owner_ref[r * n_blocks + c]
            for z in range(NZ):
                out_ref[z, owner] = total.astype(out_ref.dtype)


def halves_kernel(column_ref, low_ref, top_ref):
    n = low_ref.shape[0]
    low_ref[...] = column_ref[:n]
    top_ref[...] = column_ref[n:]


def pair_kernel(one_ref, two_ref, out_ref):
    out_ref[0] = one_ref[...]
    out_ref[1] = two_ref[...]


def root_kernel(pair_ref, swap_ref, root_ref):
    x_me = lax.axis_index("x")
    share = pair_ref.shape[1] // NZ
    for j, (ref, part) in enumerate(((pair_ref, 0), (pair_ref, 1), (swap_ref, 1), (swap_ref, 0))):
        for z in range(NZ):
            at = pl.multiple_of((z * NX + lax.bitwise_xor(x_me, j)) * share, share)
            root_ref[pl.ds(at, share), :] = ref[part, z * share : (z + 1) * share, :]


def product_kernel(*refs):
    piece_refs = refs[: 2 * NX]
    (root_ref, left_root_hbm, left_prev_hbm, right_prev_hbm, left_hbm, right_hbm, update_hbm,
     g_ref, stack_ref, left_prev, right_prev, pair_ref, both_ref, left_new, right_new, update, sems) = refs[2 * NX :]
    zh = lax.axis_index("zh")
    x_me = lax.axis_index("x")
    d = zh * NX + x_me
    share = left_prev.shape[0]
    loads = [
        pltpu.make_async_copy(a, b, sems.at[i])
        for i, (a, b) in enumerate(
            ((left_root_hbm, stack_ref.at[:share]), (left_prev_hbm, left_prev), (right_prev_hbm, right_prev))
        )
    ]
    stores = [
        pltpu.make_async_copy(a, b, sems.at[3 + i])
        for i, (a, b) in enumerate(((left_new, left_hbm), (right_new, right_hbm), (update, update_hbm)))
    ]
    for c in loads:
        c.start()
    n_half, n_piece, high, width = piece_refs[0].shape
    n_src = n_piece // NL
    for j in range(NX):
        x = lax.bitwise_xor(x_me, j)
        for z in range(NZ):
            ref = piece_refs[2 * j + z // n_half]
            for p in range(n_piece):
                at = pl.multiple_of((p % n_src * NX + x) * high, high)
                to = (z * NL + p // n_src) * width
                g_ref[pl.ds(at, high), to : to + width] = ref[z % n_half, p]
    rows = g_ref[pl.ds(pl.multiple_of(d * share, share), share), :]
    g = g_ref[...]
    left_gram = lax.dot_general(rows, g, (((1,), (1,)), ((), ())), preferred_element_type=jnp.float32)
    for c in loads:
        c.wait()
    left_new[...] = decay_rate * left_prev[...] + (1.0 - decay_rate) * left_gram
    stores[0].start()
    pair = g_ref[:, pl.ds(pl.multiple_of((d // 2) * 2 * share, 2 * share), 2 * share)]
    pair_ref[...] = pair.T
    stack_ref[share:, :] = pair_ref[pl.ds(pl.multiple_of(lax.rem(d, 2) * share, share), share), :]
    both_ref[...] = jnp.dot(stack_ref[...], g, preferred_element_type=jnp.float32)
    right_new[...] = decay_rate * right_prev[...] + (1.0 - decay_rate) * both_ref[share:, :]
    stores[1].start()
    half = both_ref[:share, :].astype(jnp.bfloat16)
    update[...] = jnp.dot(half, root_ref[...], preferred_element_type=jnp.float32).astype(update.dtype)
    stores[2].start()
    for c in stores:
        c.wait()


def on_device(partials, owner, left_prev, right_prev, left_root, right_root):
    bf16, f32 = jnp.bfloat16, jnp.float32
    part = partials[0]
    rows, cols = part.shape
    order = left_prev.shape[2]
    share = left_prev.shape[1]
    n_blocks = cols // order
    n_mp = lax.axis_size(MP)
    high = rows // NX
    width = order // (NZ * NL)
    piece = (n_blocks, high, width)
    vmem = pl.BlockSpec(memory_space=pltpu.VMEM)
    smem = pl.BlockSpec(memory_space=pltpu.SMEM)
    anywhere = pl.BlockSpec(memory_space=pl.ANY)
    shape = jax.ShapeDtypeStruct

    swaps = {k: [(i, i ^ k) for i in range(NX)] for k in range(1, NX)}

    root_z = lax.all_gather(right_root[0], "zh", tiled=True)
    got = lax.all_to_all(part.reshape(NX, high, cols), "x", 0, 0, tiled=True)
    got, root_z = lax.optimization_barrier((got, root_z))
    cut = 1
    sums = call(
        sum_x_kernel,
        shape((NZ * NL,) + piece, bf16),
        grid=(cut,),
        in_specs=[pl.BlockSpec((NX, high, cols), lambda i: (0, 0, 0))],
        out_specs=pl.BlockSpec((NZ * NL // cut,) + piece, lambda i: (i, 0, 0, 0)),
    )(got)
    root_next = lax.ppermute(root_z, "x", swaps[1])
    got = lax.all_to_all(sums, ("zh", "zl"), 0, 0, tiled=True)
    got, root_z, root_next = lax.optimization_barrier((got, root_z, root_next))
    routed = call(
        route_kernel, shape((NZ, n_mp, high, width), bf16), in_specs=[smem, vmem], out_specs=vmem
    )(owner, got)
    root_pair = call(
        pair_kernel, shape((2,) + root_z.shape, bf16), in_specs=[vmem, vmem], out_specs=vmem
    )(root_z, root_next)
    routed, root_pair = lax.optimization_barrier((routed, root_pair))
    root_swap = lax.ppermute(root_pair, "x", swaps[3])
    column = lax.all_to_all(routed.reshape((NZ * n_mp,) + piece[1:]), ("zh",) + MP, 0, 0, tiled=True)
    column = column.reshape((NZ, n_mp) + piece[1:])
    column, root_swap = lax.optimization_barrier((column, root_swap))
    low, top = call(
        halves_kernel, (shape((NZ // 2,) + column.shape[1:], bf16),) * 2, in_specs=[vmem], out_specs=(vmem, vmem)
    )(column)
    low_1 = lax.ppermute(low, "x", swaps[1])
    top_3 = lax.ppermute(top, "x", swaps[3])
    top_1 = lax.ppermute(top, "x", swaps[1])
    low_3 = lax.ppermute(low, "x", swaps[3])
    low_2 = lax.ppermute(low_1, "x", swaps[3])
    top_2 = lax.ppermute(top_3, "x", swaps[1])
    pieces = [low, top, low_1, top_1, low_2, top_2, low_3, top_3]
    root = call(root_kernel, shape((order, order), bf16), in_specs=[vmem, vmem], out_specs=vmem)(root_pair, root_swap)
    left_new, right_new, update = call(
        product_kernel,
        (shape((share, order), f32), shape((share, order), f32), shape((share, order), bf16)),
        in_specs=[vmem] * (2 * NX + 1) + [anywhere] * 3,
        out_specs=(anywhere, anywhere, anywhere),
        scratch_shapes=[
            pltpu.VMEM((order, order), bf16),
            pltpu.VMEM((2 * share, order), bf16),
            pltpu.VMEM((share, order), f32),
            pltpu.VMEM((share, order), f32),
            pltpu.VMEM((2 * share, order), bf16),
            pltpu.VMEM((2 * share, order), f32),
            pltpu.VMEM((share, order), f32),
            pltpu.VMEM((share, order), f32),
            pltpu.VMEM((share, order), bf16),
            pltpu.SemaphoreType.DMA((6,)),
        ],
    )(*pieces, root, left_root[0], left_prev[0], right_prev[0])
    return left_new[None], right_new[None], update[None]


def solution(mesh):
    cut = Mesh(mesh.devices.reshape(NZ, NX, 2, 8, 2), DP + MP)
    spread = P(MP, DP, None)
    return jax.shard_map(
        on_device,
        mesh=cut,
        in_specs=(P(DP, MP, None), P(), spread, spread, spread, spread),
        out_specs=(spread, spread, spread),
        check_vma=False,
    )
```

```python
import jax
import jax.numpy as jnp
from jax import lax
from jax.experimental import pallas as pl
from jax.experimental.pallas import tpu as pltpu
from jax.sharding import Mesh
from jax.sharding import PartitionSpec as P

decay_rate = 0.95
DP = ("zh", "x")
MP = ("zl", "y", "c")
NX = 4
NZ = 4
NL = 2
VMEM_LIMIT = 32 * 1024 * 1024


def call(kernel, out_shape, **kw):
    return pl.pallas_call(
        kernel,
        out_shape=out_shape,
        compiler_params=pltpu.CompilerParams(vmem_limit_bytes=VMEM_LIMIT),
        **kw,
    )


def sum_x_kernel(got_ref, out_ref):
    n_here, n_blocks, _, width = out_ref.shape
    first = pl.program_id(0) * n_here
    for c in range(n_blocks):
        for z in range(n_here):
            cols = pl.ds(pl.multiple_of((c * NZ * NL + first + z) * width, width), width)
            total = got_ref[0, :, cols].astype(jnp.float32)
            for src in range(1, NX):
                total += got_ref[src, :, cols].astype(jnp.float32)
            out_ref[z, c] = total.astype(out_ref.dtype)


def route_kernel(owner_ref, got_ref, out_ref):
    n_blocks = got_ref.shape[1]
    for r in range(NL):
        for c in range(n_blocks):
            total = got_ref[r * NZ, c].astype(jnp.float32)
            for src in range(1, NZ):
                total += got_ref[r * NZ + src, c].astype(jnp.float32)
            owner = owner_ref[r * n_blocks + c]
            for z in range(NZ):
                out_ref[owner, z] = total.astype(out_ref.dtype)


def halves_kernel(column_ref, low_ref, top_ref):
    n = low_ref.shape[0]
    low_ref[...] = column_ref[:n]
    top_ref[...] = column_ref[n:]


def pair_kernel(one_ref, two_ref, out_ref):
    out_ref[0] = one_ref[...]
    out_ref[1] = two_ref[...]


def root_kernel(pair_ref, swap_ref, root_ref):
    x_me = lax.axis_index("x")
    share = pair_ref.shape[1] // NZ
    for j, (ref, part) in enumerate(((pair_ref, 0), (pair_ref, 1), (swap_ref, 1), (swap_ref, 0))):
        for z in range(NZ):
            at = pl.multiple_of((z * NX + lax.bitwise_xor(x_me, j)) * share, share)
            root_ref[pl.ds(at, share), :] = ref[part, z * share : (z + 1) * share, :]


def product_kernel(*refs):
    piece_refs = refs[: 2 * NX]
    (root_ref, left_root_hbm, left_prev_hbm, right_prev_hbm, left_hbm, right_hbm, update_hbm,
     g_ref, stack_ref, left_prev, right_prev, pair_ref, both_ref, left_new, right_new, update, sems) = refs[2 * NX :]
    zh = lax.axis_index("zh")
    x_me = lax.axis_index("x")
    d = zh * NX + x_me
    share = left_prev.shape[0]
    loads = [
        pltpu.make_async_copy(a, b, sems.at[i])
        for i, (a, b) in enumerate(
            ((left_root_hbm, stack_ref.at[:share]), (left_prev_hbm, left_prev), (right_prev_hbm, right_prev))
        )
    ]
    stores = [
        pltpu.make_async_copy(a, b, sems.at[3 + i])
        for i, (a, b) in enumerate(((left_new, left_hbm), (right_new, right_hbm), (update, update_hbm)))
    ]
    for c in loads:
        c.start()
    n_src, _, high, width = piece_refs[0].shape
    for j in range(NX):
        x = lax.bitwise_xor(x_me, j)
        for half in range(NL):
            for s in range(n_src):
                at = pl.multiple_of((s * NX + x) * high, high)
                for z in range(NZ):
                    to = (half * NZ + z) * width
                    g_ref[pl.ds(at, high), to : to + width] = piece_refs[2 * j + half][s, z]
    rows = g_ref[pl.ds(pl.multiple_of(d * share, share), share), :]
    g = g_ref[...]
    left_gram = lax.dot_general(rows, g, (((1,), (1,)), ((), ())), preferred_element_type=jnp.float32)
    for c in loads:
        c.wait()
    left_new[...] = decay_rate * left_prev[...] + (1.0 - decay_rate) * left_gram
    stores[0].start()
    pair = g_ref[:, pl.ds(pl.multiple_of((d // 2) * 2 * share, 2 * share), 2 * share)]
    pair_ref[...] = pair.T
    stack_ref[share:, :] = pair_ref[pl.ds(pl.multiple_of(lax.rem(d, 2) * share, share), share), :]
    both_ref[...] = jnp.dot(stack_ref[...], g, preferred_element_type=jnp.float32)
    right_new[...] = decay_rate * right_prev[...] + (1.0 - decay_rate) * both_ref[share:, :]
    stores[1].start()
    half = both_ref[:share, :].astype(jnp.bfloat16)
    update[...] = jnp.dot(half, root_ref[...], preferred_element_type=jnp.float32).astype(update.dtype)
    stores[2].start()
    for c in stores:
        c.wait()


def on_device(partials, owner, left_prev, right_prev, left_root, right_root):
    bf16, f32 = jnp.bfloat16, jnp.float32
    part = partials[0]
    rows, cols = part.shape
    order = left_prev.shape[2]
    share = left_prev.shape[1]
    n_blocks = cols // order
    n_mp = lax.axis_size(MP)
    high = rows // NX
    width = order // (NZ * NL)
    piece = (n_blocks, high, width)
    vmem = pl.BlockSpec(memory_space=pltpu.VMEM)
    smem = pl.BlockSpec(memory_space=pltpu.SMEM)
    anywhere = pl.BlockSpec(memory_space=pl.ANY)
    shape = jax.ShapeDtypeStruct

    swaps = {k: [(i, i ^ k) for i in range(NX)] for k in range(1, NX)}

    root_z = lax.all_gather(right_root[0], "zh", tiled=True)
    got = lax.all_to_all(part.reshape(NX, high, cols), "x", 0, 0, tiled=True)
    got, root_z = lax.optimization_barrier((got, root_z))
    cut = 1
    sums = call(
        sum_x_kernel,
        shape((NZ * NL,) + piece, bf16),
        grid=(cut,),
        in_specs=[pl.BlockSpec((NX, high, cols), lambda i: (0, 0, 0))],
        out_specs=pl.BlockSpec((NZ * NL // cut,) + piece, lambda i: (i, 0, 0, 0)),
    )(got)
    root_next = lax.ppermute(root_z, "x", swaps[1])
    got = lax.all_to_all(sums, ("zl", "zh"), 0, 0, tiled=True)
    got, root_z, root_next = lax.optimization_barrier((got, root_z, root_next))
    routed = call(
        route_kernel, shape((n_mp, NZ, high, width), bf16), in_specs=[smem, vmem], out_specs=vmem
    )(owner, got)
    root_pair = call(
        pair_kernel, shape((2,) + root_z.shape, bf16), in_specs=[vmem, vmem], out_specs=vmem
    )(root_z, root_next)
    routed, root_pair = lax.optimization_barrier((routed, root_pair))
    root_swap = lax.ppermute(root_pair, "x", swaps[3])
    column = lax.all_to_all(routed.reshape((n_mp * NZ,) + piece[1:]), MP + ("zh",), 0, 0, tiled=True)
    column = column.reshape((n_mp, NZ) + piece[1:])
    column, root_swap = lax.optimization_barrier((column, root_swap))
    low, top = call(
        halves_kernel, (shape((n_mp // 2,) + column.shape[1:], bf16),) * 2, in_specs=[vmem], out_specs=(vmem, vmem)
    )(column)
    low_1 = lax.ppermute(low, "x", swaps[1])
    top_3 = lax.ppermute(top, "x", swaps[3])
    top_1 = lax.ppermute(top, "x", swaps[1])
    low_3 = lax.ppermute(low, "x", swaps[3])
    low_2 = lax.ppermute(low_1, "x", swaps[3])
    top_2 = lax.ppermute(top_3, "x", swaps[1])
    pieces = [low, top, low_1, top_1, low_2, top_2, low_3, top_3]
    root = call(root_kernel, shape((order, order), bf16), in_specs=[vmem, vmem], out_specs=vmem)(root_pair, root_swap)
    left_new, right_new, update = call(
        product_kernel,
        (shape((share, order), f32), shape((share, order), f32), shape((share, order), bf16)),
        in_specs=[vmem] * (2 * NX + 1) + [anywhere] * 3,
        out_specs=(anywhere, anywhere, anywhere),
        scratch_shapes=[
            pltpu.VMEM((order, order), bf16),
            pltpu.VMEM((2 * share, order), bf16),
            pltpu.VMEM((share, order), f32),
            pltpu.VMEM((share, order), f32),
            pltpu.VMEM((2 * share, order), bf16),
            pltpu.VMEM((2 * share, order), f32),
            pltpu.VMEM((share, order), f32),
            pltpu.VMEM((share, order), f32),
            pltpu.VMEM((share, order), bf16),
            pltpu.SemaphoreType.DMA((6,)),
        ],
    )(*pieces, root, left_root[0], left_prev[0], right_prev[0])
    return left_new[None], right_new[None], update[None]


def solution(mesh):
    cut = Mesh(mesh.devices.reshape(NZ, NX, 2, 8, 2), DP + MP)
    spread = P(MP, DP, None)
    return jax.shard_map(
        on_device,
        mesh=cut,
        in_specs=(P(DP, MP, None), P(), spread, spread, spread, spread),
        out_specs=(spread, spread, spread),
        check_vma=False,
    )
```

```python
import jax
import jax.numpy as jnp
from jax import lax
from jax.experimental import pallas as pl
from jax.experimental.pallas import tpu as pltpu
from jax.sharding import Mesh
from jax.sharding import PartitionSpec as P

decay_rate = 0.95
DP = ("zh", "x")
MP = ("zl", "y", "c")
NX = 4
NZ = 4
NL = 2
VMEM_LIMIT = 32 * 1024 * 1024


def call(kernel, out_shape, **kw):
    return pl.pallas_call(
        kernel,
        out_shape=out_shape,
        compiler_params=pltpu.CompilerParams(vmem_limit_bytes=VMEM_LIMIT),
        **kw,
    )


def sum_x_kernel(got_ref, out_ref):
    n_here, n_blocks, _, width = out_ref.shape
    first = pl.program_id(0) * n_here
    for c in range(n_blocks):
        for z in range(n_here):
            cols = pl.ds(pl.multiple_of((c * NZ * NL + first + z) * width, width), width)
            total = got_ref[0, :, cols].astype(jnp.float32)
            for src in range(1, NX):
                total += got_ref[src, :, cols].astype(jnp.float32)
            out_ref[z, c] = total.astype(out_ref.dtype)


def route_kernel(owner_ref, got_ref, out_ref):
    n_blocks = got_ref.shape[1]
    for r in range(NL):
        for c in range(n_blocks):
            total = got_ref[r * NZ, c].astype(jnp.float32)
            for src in range(1, NZ):
                total += got_ref[r * NZ + src, c].astype(jnp.float32)
            owner = owner_ref[r * n_blocks + c]
            for z in range(NZ):
                out_ref[owner, z] = total.astype(out_ref.dtype)


def halves_kernel(column_ref, rest_ref, low_ref, top_ref):
    n = column_ref.shape[0] // 2
    high = column_ref.shape[2]
    deep = rest_ref.shape[0] // 2
    for i, ref in enumerate((low_ref, top_ref)):
        ref[:n] = column_ref[i * n : (i + 1) * n]
        for u in range(deep // high):
            ref[n + u // NZ, u % NZ] = rest_ref[i * deep + u * high : i * deep + (u + 1) * high, :]


def root_kernel(a_ref, b_ref, root_ref):
    share = a_ref.shape[1] * 2 // NZ
    for x in range(NX):
        for z in range(NZ):
            ref, at = (a_ref, z) if z < NZ // 2 else (b_ref, z - NZ // 2)
            root_ref[(z * NX + x) * share : (z * NX + x + 1) * share, :] = ref[x, at * share : (at + 1) * share, :]


def product_kernel(*refs):
    piece_refs = refs[: 2 * NX]
    (root_ref, left_root_hbm, left_prev_hbm, right_prev_hbm, left_hbm, right_hbm, update_hbm,
     g_ref, rest_ref, stack_ref, left_prev, right_prev, pair_ref, both_ref, left_new, right_new, update, sems) = refs[2 * NX :]
    zh = lax.axis_index("zh")
    x_me = lax.axis_index("x")
    d = zh * NX + x_me
    share = left_prev.shape[0]
    loads = [
        pltpu.make_async_copy(a, b, sems.at[i])
        for i, (a, b) in enumerate(
            ((left_root_hbm, stack_ref.at[:share]), (left_prev_hbm, left_prev), (right_prev_hbm, right_prev))
        )
    ]
    stores = [
        pltpu.make_async_copy(a, b, sems.at[3 + i])
        for i, (a, b) in enumerate(((left_new, left_hbm), (right_new, right_hbm), (update, update_hbm)))
    ]
    for c in loads:
        c.start()
    n_src = g_ref.shape[0] // (NX * piece_refs[0].shape[2])
    high, width = piece_refs[0].shape[2:]
    per = share // high
    main = root_ref.shape[1]
    for j in range(NX):
        x = lax.bitwise_xor(x_me, j)
        for half in range(NL):
            for s in range(n_src):
                at = pl.multiple_of((s * NX + x) * high, high)
                for z in range(NZ):
                    to = (half * NZ + z) * width
                    g_ref[pl.ds(at, high), to : to + width] = piece_refs[2 * j + half][s, z]
            for u in range(NZ // 2 * per):
                at = pl.multiple_of(((half * NZ // 2 + u // per) * NX + x) * share + u % per * high, high)
                rest_ref[pl.ds(at, high), :] = piece_refs[2 * j + half][n_src + u // NZ, u % NZ]
    rows = g_ref[pl.ds(pl.multiple_of(d * share, share), share), :]
    g = g_ref[...]
    left_gram = lax.dot_general(rows, g, (((1,), (1,)), ((), ())), preferred_element_type=jnp.float32)
    for c in loads:
        c.wait()
    left_new[...] = decay_rate * left_prev[...] + (1.0 - decay_rate) * left_gram
    stores[0].start()
    pair = g_ref[:, pl.ds(pl.multiple_of((d // 2) * 2 * share, 2 * share), 2 * share)]
    pair_ref[...] = pair.T
    stack_ref[share:, :] = pair_ref[pl.ds(pl.multiple_of(lax.rem(d, 2) * share, share), share), :]
    both_ref[...] = jnp.dot(stack_ref[...], g, preferred_element_type=jnp.float32)
    right_new[...] = decay_rate * right_prev[...] + (1.0 - decay_rate) * both_ref[share:, :]
    stores[1].start()
    half = both_ref[:share, :].astype(jnp.bfloat16)
    update[:, :main] = jnp.dot(half, root_ref[...], preferred_element_type=jnp.float32).astype(update.dtype)
    update[:, main:] = jnp.dot(half, rest_ref[...], preferred_element_type=jnp.float32).astype(update.dtype)
    stores[2].start()
    for c in stores:
        c.wait()


def on_device(partials, owner, left_prev, right_prev, left_root, right_root):
    bf16, f32 = jnp.bfloat16, jnp.float32
    part = partials[0]
    rows, cols = part.shape
    order = left_prev.shape[2]
    share = left_prev.shape[1]
    n_blocks = cols // order
    n_mp = lax.axis_size(MP)
    high = rows // NX
    width = order // (NZ * NL)
    piece = (n_blocks, high, width)
    vmem = pl.BlockSpec(memory_space=pltpu.VMEM)
    smem = pl.BlockSpec(memory_space=pltpu.SMEM)
    anywhere = pl.BlockSpec(memory_space=pl.ANY)
    shape = jax.ShapeDtypeStruct

    swaps = {k: [(i, i ^ k) for i in range(NX)] for k in range(1, NX)}

    root_z = lax.all_gather(right_root[0], "zh", tiled=True)
    got = lax.all_to_all(part.reshape(NX, high, cols), "x", 0, 0, tiled=True)
    got, root_z = lax.optimization_barrier((got, root_z))
    deep, main = NZ * share // 2, order - width
    root_a, root_b, root_rest = root_z[:deep, :main], root_z[deep:, :main], root_z[:, main:]
    cut = 1
    sums = call(
        sum_x_kernel,
        shape((NZ * NL,) + piece, bf16),
        grid=(cut,),
        in_specs=[pl.BlockSpec((NX, high, cols), lambda i: (0, 0, 0))],
        out_specs=pl.BlockSpec((NZ * NL // cut,) + piece, lambda i: (i, 0, 0, 0)),
    )(got)
    sums, root_a, root_b, root_rest = lax.optimization_barrier((sums, root_a, root_b, root_rest))
    root_a = lax.all_gather(root_a, "x")
    got = lax.all_to_all(sums, ("zl", "zh"), 0, 0, tiled=True)
    got, root_a, root_b = lax.optimization_barrier((got, root_a, root_b))
    routed = call(
        route_kernel, shape((n_mp, NZ, high, width), bf16), in_specs=[smem, vmem], out_specs=vmem
    )(owner, got)
    routed, root_b = lax.optimization_barrier((routed, root_b))
    root_b = lax.all_gather(root_b, "x")
    column = lax.all_to_all(routed.reshape((n_mp * NZ,) + piece[1:]), MP + ("zh",), 0, 0, tiled=True)
    column = column.reshape((n_mp, NZ) + piece[1:])
    column, root_b = lax.optimization_barrier((column, root_b))
    n_half = n_mp // 2 + deep // (NZ * high)
    low, top = call(
        halves_kernel, (shape((n_half,) + column.shape[1:], bf16),) * 2, in_specs=[vmem] * 2, out_specs=(vmem, vmem)
    )(column, root_rest)
    low_1 = lax.ppermute(low, "x", swaps[1])
    top_3 = lax.ppermute(top, "x", swaps[3])
    top_1 = lax.ppermute(top, "x", swaps[1])
    low_3 = lax.ppermute(low, "x", swaps[3])
    low_2 = lax.ppermute(low_1, "x", swaps[3])
    top_2 = lax.ppermute(top_3, "x", swaps[1])
    pieces = [low, top, low_1, top_1, low_2, top_2, low_3, top_3]
    root = call(root_kernel, shape((order, main), bf16), in_specs=[vmem] * 2, out_specs=vmem)(root_a, root_b)
    left_new, right_new, update = call(
        product_kernel,
        (shape((share, order), f32), shape((share, order), f32), shape((share, order), bf16)),
        in_specs=[vmem] * (2 * NX + 1) + [anywhere] * 3,
        out_specs=(anywhere, anywhere, anywhere),
        scratch_shapes=[
            pltpu.VMEM((order, order), bf16),
            pltpu.VMEM((order, width), bf16),
            pltpu.VMEM((2 * share, order), bf16),
            pltpu.VMEM((share, order), f32),
            pltpu.VMEM((share, order), f32),
            pltpu.VMEM((2 * share, order), bf16),
            pltpu.VMEM((2 * share, order), f32),
            pltpu.VMEM((share, order), f32),
            pltpu.VMEM((share, order), f32),
            pltpu.VMEM((share, order), bf16),
            pltpu.SemaphoreType.DMA((6,)),
        ],
    )(*pieces, root, left_root[0], left_prev[0], right_prev[0])
    return left_new[None], right_new[None], update[None]


def solution(mesh):
    cut = Mesh(mesh.devices.reshape(NZ, NX, 2, 8, 2), DP + MP)
    spread = P(MP, DP, None)
    return jax.shard_map(
        on_device,
        mesh=cut,
        in_specs=(P(DP, MP, None), P(), spread, spread, spread, spread),
        out_specs=(spread, spread, spread),
        check_vma=False,
    )
```

```python
import jax
import jax.numpy as jnp
from jax import lax
from jax.experimental import pallas as pl
from jax.experimental.pallas import tpu as pltpu
from jax.sharding import Mesh
from jax.sharding import PartitionSpec as P

decay_rate = 0.95
DP = ("zh", "x")
MP = ("zl", "y", "c")
NX = 4
NZ = 4
NL = 2
VMEM_LIMIT = 32 * 1024 * 1024


def call(kernel, out_shape, **kw):
    return pl.pallas_call(
        kernel,
        out_shape=out_shape,
        compiler_params=pltpu.CompilerParams(vmem_limit_bytes=VMEM_LIMIT),
        **kw,
    )


def sum_x_kernel(got_ref, out_ref):
    n_here, n_blocks, _, width = out_ref.shape
    first = pl.program_id(0) * n_here
    for c in range(n_blocks):
        for z in range(n_here):
            cols = pl.ds(pl.multiple_of((c * NZ * NL + first + z) * width, width), width)
            total = got_ref[0, :, cols].astype(jnp.float32)
            for src in range(1, NX):
                total += got_ref[src, :, cols].astype(jnp.float32)
            out_ref[z, c] = total.astype(out_ref.dtype)


def route_kernel(owner_ref, got_ref, out_ref):
    n_blocks = got_ref.shape[1]
    for r in range(NL):
        for c in range(n_blocks):
            total = got_ref[r * NZ, c].astype(jnp.float32)
            for src in range(1, NZ):
                total += got_ref[r * NZ + src, c].astype(jnp.float32)
            owner = owner_ref[r * n_blocks + c]
            for z in range(NZ):
                out_ref[owner, z] = total.astype(out_ref.dtype)


def halves_kernel(column_ref, rest_ref, low_ref, top_ref):
    n = column_ref.shape[0] // 2
    high = column_ref.shape[2]
    deep = rest_ref.shape[0] // 2
    for i, ref in enumerate((low_ref, top_ref)):
        ref[:n] = column_ref[i * n : (i + 1) * n]
        for u in range(deep // high):
            ref[n + u // NZ, u % NZ] = rest_ref[i * deep + u * high : i * deep + (u + 1) * high, :]


def root_kernel(a_ref, b_ref, root_ref):
    share = a_ref.shape[1] * 2 // NZ
    for x in range(NX):
        for z in range(NZ):
            ref, at = (a_ref, z) if z < NZ // 2 else (b_ref, z - NZ // 2)
            root_ref[(z * NX + x) * share : (z * NX + x + 1) * share, :] = ref[x, at * share : (at + 1) * share, :]


def product_kernel(*refs):
    piece_refs = refs[: 2 * NX]
    (root_ref, left_root_ref, left_prev, right_prev, left_hbm, right_hbm, update_hbm,
     g_ref, rest_ref, stack_ref, pair_ref, both_ref, left_new, right_new, update, sems) = refs[2 * NX :]
    zh = lax.axis_index("zh")
    x_me = lax.axis_index("x")
    d = zh * NX + x_me
    share = left_prev.shape[0]
    stores = [
        pltpu.make_async_copy(a, b, sems.at[i])
        for i, (a, b) in enumerate(((left_new, left_hbm), (right_new, right_hbm), (update, update_hbm)))
    ]
    n_src = g_ref.shape[0] // (NX * piece_refs[0].shape[2])
    high, width = piece_refs[0].shape[2:]
    per = share // high
    main = root_ref.shape[1]
    for j in range(NX):
        x = lax.bitwise_xor(x_me, j)
        for half in range(NL):
            for s in range(n_src):
                at = pl.multiple_of((s * NX + x) * high, high)
                for z in range(NZ):
                    to = (half * NZ + z) * width
                    g_ref[pl.ds(at, high), to : to + width] = piece_refs[2 * j + half][s, z]
            for u in range(NZ // 2 * per):
                at = pl.multiple_of(((half * NZ // 2 + u // per) * NX + x) * share + u % per * high, high)
                rest_ref[pl.ds(at, high), :] = piece_refs[2 * j + half][n_src + u // NZ, u % NZ]
    rows = g_ref[pl.ds(pl.multiple_of(d * share, share), share), :]
    g = g_ref[...]
    left_gram = lax.dot_general(rows, g, (((1,), (1,)), ((), ())), preferred_element_type=jnp.float32)
    left_new[...] = decay_rate * left_prev[...] + (1.0 - decay_rate) * left_gram
    stores[0].start()
    pair = g_ref[:, pl.ds(pl.multiple_of((d // 2) * 2 * share, 2 * share), 2 * share)]
    pair_ref[...] = pair.T
    stack_ref[:share, :] = left_root_ref[...]
    stack_ref[share:, :] = pair_ref[pl.ds(pl.multiple_of(lax.rem(d, 2) * share, share), share), :]
    both_ref[...] = jnp.dot(stack_ref[...], g, preferred_element_type=jnp.float32)
    right_new[...] = decay_rate * right_prev[...] + (1.0 - decay_rate) * both_ref[share:, :]
    stores[1].start()
    half = both_ref[:share, :].astype(jnp.bfloat16)
    update[:, :main] = jnp.dot(half, root_ref[...], preferred_element_type=jnp.float32).astype(update.dtype)
    update[:, main:] = jnp.dot(half, rest_ref[...], preferred_element_type=jnp.float32).astype(update.dtype)
    stores[2].start()
    for c in stores:
        c.wait()


def on_device(partials, owner, left_prev, right_prev, left_root, right_root):
    bf16, f32 = jnp.bfloat16, jnp.float32
    part = partials[0]
    rows, cols = part.shape
    order = left_prev.shape[2]
    share = left_prev.shape[1]
    n_blocks = cols // order
    n_mp = lax.axis_size(MP)
    high = rows // NX
    width = order // (NZ * NL)
    piece = (n_blocks, high, width)
    vmem = pl.BlockSpec(memory_space=pltpu.VMEM)
    smem = pl.BlockSpec(memory_space=pltpu.SMEM)
    anywhere = pl.BlockSpec(memory_space=pl.ANY)
    shape = jax.ShapeDtypeStruct

    swaps = {k: [(i, i ^ k) for i in range(NX)] for k in range(1, NX)}

    root_z = lax.all_gather(right_root[0], "zh", tiled=True)
    got = lax.all_to_all(part.reshape(NX, high, cols), "x", 0, 0, tiled=True)
    got, root_z = lax.optimization_barrier((got, root_z))
    deep, main = NZ * share // 2, order - width
    root_a, root_b, root_rest = root_z[:deep, :main], root_z[deep:, :main], root_z[:, main:]
    cut = 1
    sums = call(
        sum_x_kernel,
        shape((NZ * NL,) + piece, bf16),
        grid=(cut,),
        in_specs=[pl.BlockSpec((NX, high, cols), lambda i: (0, 0, 0))],
        out_specs=pl.BlockSpec((NZ * NL // cut,) + piece, lambda i: (i, 0, 0, 0)),
    )(got)
    sums, root_a, root_b, root_rest = lax.optimization_barrier((sums, root_a, root_b, root_rest))
    root_a = lax.all_gather(root_a, "x")
    got = lax.all_to_all(sums, ("zl", "zh"), 0, 0, tiled=True)
    got, root_a, root_b = lax.optimization_barrier((got, root_a, root_b))
    routed = call(
        route_kernel, shape((n_mp, NZ, high, width), bf16), in_specs=[smem, vmem], out_specs=vmem
    )(owner, got)
    routed, root_b = lax.optimization_barrier((routed, root_b))
    root_b = lax.all_gather(root_b, "x")
    column = lax.all_to_all(routed.reshape((n_mp * NZ,) + piece[1:]), MP + ("zh",), 0, 0, tiled=True)
    column = column.reshape((n_mp, NZ) + piece[1:])
    column, root_b = lax.optimization_barrier((column, root_b))
    n_half = n_mp // 2 + deep // (NZ * high)
    low, top = call(
        halves_kernel, (shape((n_half,) + column.shape[1:], bf16),) * 2, in_specs=[vmem] * 2, out_specs=(vmem, vmem)
    )(column, root_rest)
    low_1 = lax.ppermute(low, "x", swaps[1])
    top_3 = lax.ppermute(top, "x", swaps[3])
    top_1 = lax.ppermute(top, "x", swaps[1])
    low_3 = lax.ppermute(low, "x", swaps[3])
    low_2 = lax.ppermute(low_1, "x", swaps[3])
    top_2 = lax.ppermute(top_3, "x", swaps[1])
    pieces = [low, top, low_1, top_1, low_2, top_2, low_3, top_3]
    root = call(root_kernel, shape((order, main), bf16), in_specs=[vmem] * 2, out_specs=vmem)(root_a, root_b)
    left_new, right_new, update = call(
        product_kernel,
        (shape((share, order), f32), shape((share, order), f32), shape((share, order), bf16)),
        in_specs=[vmem] * (2 * NX + 4),
        out_specs=(anywhere, anywhere, anywhere),
        scratch_shapes=[
            pltpu.VMEM((order, order), bf16),
            pltpu.VMEM((order, width), bf16),
            pltpu.VMEM((2 * share, order), bf16),
            pltpu.VMEM((2 * share, order), bf16),
            pltpu.VMEM((2 * share, order), f32),
            pltpu.VMEM((share, order), f32),
            pltpu.VMEM((share, order), f32),
            pltpu.VMEM((share, order), bf16),
            pltpu.SemaphoreType.DMA((3,)),
        ],
    )(*pieces, root, left_root[0], left_prev[0], right_prev[0])
    return left_new[None], right_new[None], update[None]


def solution(mesh):
    cut = Mesh(mesh.devices.reshape(NZ, NX, 2, 8, 2), DP + MP)
    spread = P(MP, DP, None)
    return jax.shard_map(
        on_device,
        mesh=cut,
        in_specs=(P(DP, MP, None), P(), spread, spread, spread, spread),
        out_specs=(spread, spread, spread),
        check_vma=False,
    )
```

```python
import jax
import jax.numpy as jnp
from jax import lax
from jax.experimental import pallas as pl
from jax.experimental.pallas import tpu as pltpu
from jax.sharding import Mesh
from jax.sharding import PartitionSpec as P

decay_rate = 0.95
DP = ("zh", "x")
MP = ("zl", "y", "c")
NX = 4
NZ = 4
NL = 2
VMEM_LIMIT = 32 * 1024 * 1024


def call(kernel, out_shape, **kw):
    return pl.pallas_call(
        kernel,
        out_shape=out_shape,
        compiler_params=pltpu.CompilerParams(vmem_limit_bytes=VMEM_LIMIT),
        **kw,
    )


def sum_x_kernel(got_ref, out_ref):
    n_here, n_blocks, _, width = out_ref.shape
    first = pl.program_id(0) * n_here
    for c in range(n_blocks):
        for z in range(n_here):
            cols = pl.ds(pl.multiple_of((c * NZ * NL + first + z) * width, width), width)
            total = got_ref[0, :, cols].astype(jnp.float32)
            for src in range(1, NX):
                total += got_ref[src, :, cols].astype(jnp.float32)
            out_ref[z, c] = total.astype(out_ref.dtype)


def route_kernel(owner_ref, got_ref, out_ref):
    n_blocks = got_ref.shape[1]
    for r in range(NL):
        for c in range(n_blocks):
            total = got_ref[r * NZ, c].astype(jnp.float32)
            for src in range(1, NZ):
                total += got_ref[r * NZ + src, c].astype(jnp.float32)
            owner = owner_ref[r * n_blocks + c]
            for z in range(NZ):
                out_ref[owner, z] = total.astype(out_ref.dtype)


def halves_kernel(column_ref, rest_ref, low_ref, top_ref):
    n = column_ref.shape[0] // 2
    high = column_ref.shape[2]
    deep = rest_ref.shape[0] // 2
    for i, ref in enumerate((low_ref, top_ref)):
        ref[:n] = column_ref[i * n : (i + 1) * n]
        for u in range(deep // high):
            ref[n + u // NZ, u % NZ] = rest_ref[i * deep + u * high : i * deep + (u + 1) * high, :]


def root_kernel(a_ref, b_ref, root_ref):
    share = a_ref.shape[1] * 2 // NZ
    for x in range(NX):
        for z in range(NZ):
            ref, at = (a_ref, z) if z < NZ // 2 else (b_ref, z - NZ // 2)
            root_ref[(z * NX + x) * share : (z * NX + x + 1) * share, :] = ref[x, at * share : (at + 1) * share, :]


def product_kernel(*refs):
    piece_refs = refs[: 2 * NX]
    (root_ref, left_root_ref, left_prev, right_prev, left_hbm, right_hbm, update_hbm,
     g_ref, rest_ref, stack_ref, pair_ref, both_ref, left_new, right_new, update, sems) = refs[2 * NX :]
    zh = lax.axis_index("zh")
    x_me = lax.axis_index("x")
    d = zh * NX + x_me
    share = left_prev.shape[0]
    stores = [
        pltpu.make_async_copy(a, b, sems.at[i])
        for i, (a, b) in enumerate(((left_new, left_hbm), (right_new, right_hbm), (update, update_hbm)))
    ]
    n_src = g_ref.shape[0] // (NX * piece_refs[0].shape[2])
    high, width = piece_refs[0].shape[2:]
    per = share // high
    main = root_ref.shape[1]
    for j in range(NX):
        x = lax.bitwise_xor(x_me, j)
        for half in range(NL):
            for s in range(n_src):
                at = pl.multiple_of((s * NX + x) * high, high)
                for z in range(NZ):
                    to = (half * NZ + z) * width
                    g_ref[pl.ds(at, high), to : to + width] = piece_refs[2 * j + half][s, z]
            for u in range(NZ // 2 * per):
                at = pl.multiple_of(((half * NZ // 2 + u // per) * NX + x) * share + u % per * high, high)
                rest_ref[pl.ds(at, high), :] = piece_refs[2 * j + half][n_src + u // NZ, u % NZ]
    g = g_ref[...]
    pair = g_ref[:, pl.ds(pl.multiple_of((d // 2) * 2 * share, 2 * share), 2 * share)]
    pair_ref[...] = pair.T
    stack_ref[:share, :] = left_root_ref[...]
    stack_ref[share:, :] = pair_ref[pl.ds(pl.multiple_of(lax.rem(d, 2) * share, share), share), :]
    both_ref[...] = jnp.dot(stack_ref[...], g, preferred_element_type=jnp.float32)
    right_new[...] = decay_rate * right_prev[...] + (1.0 - decay_rate) * both_ref[share:, :]
    stores[1].start()
    rows = g_ref[pl.ds(pl.multiple_of(d * share, share), share), :]
    left_gram = lax.dot_general(rows, g, (((1,), (1,)), ((), ())), preferred_element_type=jnp.float32)
    left_new[...] = decay_rate * left_prev[...] + (1.0 - decay_rate) * left_gram
    stores[0].start()
    half = both_ref[:share, :].astype(jnp.bfloat16)
    update[:, :main] = jnp.dot(half, root_ref[...], preferred_element_type=jnp.float32).astype(update.dtype)
    update[:, main:] = jnp.dot(half, rest_ref[...], preferred_element_type=jnp.float32).astype(update.dtype)
    stores[2].start()
    for c in stores:
        c.wait()


def on_device(partials, owner, left_prev, right_prev, left_root, right_root):
    bf16, f32 = jnp.bfloat16, jnp.float32
    part = partials[0]
    rows, cols = part.shape
    order = left_prev.shape[2]
    share = left_prev.shape[1]
    n_blocks = cols // order
    n_mp = lax.axis_size(MP)
    high = rows // NX
    width = order // (NZ * NL)
    piece = (n_blocks, high, width)
    vmem = pl.BlockSpec(memory_space=pltpu.VMEM)
    smem = pl.BlockSpec(memory_space=pltpu.SMEM)
    anywhere = pl.BlockSpec(memory_space=pl.ANY)
    shape = jax.ShapeDtypeStruct

    swaps = {k: [(i, i ^ k) for i in range(NX)] for k in range(1, NX)}

    root_z = lax.all_gather(right_root[0], "zh", tiled=True)
    got = lax.all_to_all(part.reshape(NX, high, cols), "x", 0, 0, tiled=True)
    got, root_z = lax.optimization_barrier((got, root_z))
    deep, main = NZ * share // 2, order - width
    root_a, root_b, root_rest = root_z[:deep, :main], root_z[deep:, :main], root_z[:, main:]
    cut = 1
    sums = call(
        sum_x_kernel,
        shape((NZ * NL,) + piece, bf16),
        grid=(cut,),
        in_specs=[pl.BlockSpec((NX, high, cols), lambda i: (0, 0, 0))],
        out_specs=pl.BlockSpec((NZ * NL // cut,) + piece, lambda i: (i, 0, 0, 0)),
    )(got)
    sums, root_a, root_b, root_rest = lax.optimization_barrier((sums, root_a, root_b, root_rest))
    root_a = lax.all_gather(root_a, "x")
    got = lax.all_to_all(sums, ("zl", "zh"), 0, 0, tiled=True)
    got, root_a, root_b = lax.optimization_barrier((got, root_a, root_b))
    routed = call(
        route_kernel, shape((n_mp, NZ, high, width), bf16), in_specs=[smem, vmem], out_specs=vmem
    )(owner, got)
    routed, root_b = lax.optimization_barrier((routed, root_b))
    root_b = lax.all_gather(root_b, "x")
    column = lax.all_to_all(routed.reshape((n_mp * NZ,) + piece[1:]), MP + ("zh",), 0, 0, tiled=True)
    column = column.reshape((n_mp, NZ) + piece[1:])
    column, root_b = lax.optimization_barrier((column, root_b))
    n_half = n_mp // 2 + deep // (NZ * high)
    low, top = call(
        halves_kernel, (shape((n_half,) + column.shape[1:], bf16),) * 2, in_specs=[vmem] * 2, out_specs=(vmem, vmem)
    )(column, root_rest)
    low_1 = lax.ppermute(low, "x", swaps[1])
    top_3 = lax.ppermute(top, "x", swaps[3])
    top_1 = lax.ppermute(top, "x", swaps[1])
    low_3 = lax.ppermute(low, "x", swaps[3])
    low_2 = lax.ppermute(low_1, "x", swaps[3])
    top_2 = lax.ppermute(top_3, "x", swaps[1])
    pieces = [low, top, low_1, top_1, low_2, top_2, low_3, top_3]
    root = call(root_kernel, shape((order, main), bf16), in_specs=[vmem] * 2, out_specs=vmem)(root_a, root_b)
    left_new, right_new, update = call(
        product_kernel,
        (shape((share, order), f32), shape((share, order), f32), shape((share, order), bf16)),
        in_specs=[vmem] * (2 * NX + 4),
        out_specs=(anywhere, anywhere, anywhere),
        scratch_shapes=[
            pltpu.VMEM((order, order), bf16),
            pltpu.VMEM((order, width), bf16),
            pltpu.VMEM((2 * share, order), bf16),
            pltpu.VMEM((2 * share, order), bf16),
            pltpu.VMEM((2 * share, order), f32),
            pltpu.VMEM((share, order), f32),
            pltpu.VMEM((share, order), f32),
            pltpu.VMEM((share, order), bf16),
            pltpu.SemaphoreType.DMA((3,)),
        ],
    )(*pieces, root, left_root[0], left_prev[0], right_prev[0])
    return left_new[None], right_new[None], update[None]


def solution(mesh):
    cut = Mesh(mesh.devices.reshape(NZ, NX, 2, 8, 2), DP + MP)
    spread = P(MP, DP, None)
    return jax.shard_map(
        on_device,
        mesh=cut,
        in_specs=(P(DP, MP, None), P(), spread, spread, spread, spread),
        out_specs=(spread, spread, spread),
        check_vma=False,
    )
```
